256 devices in a mesh: shot: 8 (over z), rec: 32 (over y, x, core).
Axes of the slice: x: 4, y: 4, z: 8, core: 2. Of those that a mesh axis runs over, the one named last changes fastest.
Arguments:
- primaries: bfloat16 [2, 4, 2048, 4096], P(None, None, 'shot', 'rec'), may hold values from -0.0625 to 0.0625
- recorded: bfloat16 [2, 4, 4096, 4096], P(None, None, 'shot', 'rec'), may hold values from -6 to 6
Outputs:
- multiples: float32 [2, 4, 2048, 4096], P(None, None, 'shot', 'rec')
The draws below stay inside these ranges and needn't reach their ends.
All inputs are finite; a program needn't handle non-finite values.
Results may differ from the reference program's by a relative error of at most 0.0003.
Values may be sent and summed in bfloat16 or wider, within the bound.
A program may use at most 128 MiB of HBM per device.

```python
import jax
import jax.numpy as jnp
from jax import lax

X = 4096
F = 4
S = 2048
R = 4096


def levels(stream_key, dims, shards, smallest, top_value):
    def one(dim, blocks):
        steps = jax.random.uniform(jax.random.fold_in(jax.random.fold_in(stream_key, 6), dim), (blocks,), jnp.float32, smallest / len(shards), top_value / len(shards))
        return jnp.repeat(jnp.exp(steps), dims[dim] // blocks).reshape((-1,) + (1,) * (len(dims) - dim - 1))

    loudness = one(*shards[0])
    for cut in shards[1:]:
        loudness = loudness * one(*cut)
    return loudness


def scatter_about(own_key, dims, deviation, bound, shards=(), held_as=jnp.bfloat16):
    gain = levels(own_key, dims, shards, -0.22, 0.18) if shards else 1.0
    entries = jax.random.normal(own_key, dims, jnp.float32) * deviation * gain
    return jnp.minimum(jnp.maximum(entries, -bound), bound).astype(held_as)


def setup_inputs(seed: int = 0) -> dict:
    key_list = jax.random.split(jax.random.key(seed), 3)
    return {
        "primaries": scatter_about(key_list[0], (2, F, S, X), (2 * X) ** -0.5, 0.0625, ((2, 8), (3, 32))),
        "recorded": scatter_about(key_list[1], (2, F, X, R), 1.0, 6.0, ((2, 8), (3, 32))),
    }


def product(left, right):
    return jnp.dot(left.astype(jnp.float32), right.astype(jnp.float32), precision=lax.Precision.HIGHEST, preferred_element_type=jnp.float32)


def reference(primaries, recorded):
    real_list = []
    imag_list = []
    for frequency in range(F):
        left_re = primaries[0, frequency]
        left_im = primaries[1, frequency]
        right_re = recorded[0, frequency]
        right_im = recorded[1, frequency]
        real_list.append(product(left_re, right_re) - product(left_im, right_im))
        imag_list.append(product(left_re, right_im) + product(left_im, right_re))
    return jnp.stack([jnp.stack(real_list, 0), jnp.stack(imag_list, 0)], 0)
```

```python
import jax
import jax.numpy as jnp
from jax import lax
from jax.experimental import pallas as pl
from jax.experimental.pallas import tpu as pltpu
from jax.sharding import PartitionSpec as P

MESH = pl.DeviceIdType.MESH
F = 4
NZ = 8
NQ = 16


def rec_of(x, y, c):
    return (y * 4 + x) * 2 + c


def kernel(p_ref, d_ref, o_ref, pall, dall, p_send, p_recv, sib_send, sib_recv, d_send, d_recv, local_sem):
    z = lax.axis_index("shot")
    r = lax.axis_index("rec")
    c = lax.rem(r, 2)
    x = lax.rem(r // 2, 4)
    y = r // 8
    s = lax.rem(x + y, 4)
    last, first = s // 3, (3 - s) // 3
    sibling = (z, rec_of(x, y, 1 - c))
    up, down = (lax.rem(z + 1, NZ), r), (lax.rem(z + NZ - 1, NZ), r)

    def at(dx, dy):
        return (z, rec_of(lax.rem(x + dx + 4, 4), lax.rem(y + dy + 4, 4), c))

    targets = (at(1 - last, last), at(first - 1, -first), at(last, 1 - last), at(-first, first - 1))
    place = (y * 4 + s, x * 4 + s)

    def owner(ring, k):
        i = lax.rem(place[ring // 2] + (NQ - k if ring % 2 == 0 else k), NQ)
        major = i // 4
        minor = lax.rem(lax.rem(i, 4) - major + 4, 4)
        return rec_of(minor, major, c) if ring < 2 else rec_of(major, minor, c)

    barrier = pltpu.get_barrier_semaphore()
    for other in (up, down, sibling) + targets:
        pl.semaphore_signal(barrier, inc=1, device_id=other, device_id_type=MESH)
    pl.semaphore_wait(barrier, 7)

    def d_copy(direction, source, slot, chunk):
        f = chunk // 2 if direction == 0 else 3 - chunk // 2
        part = lax.rem(chunk, 2)
        src = d_ref.at[part, f] if source is None else dall.at[source, part, f]
        return pltpu.make_async_remote_copy(
            src_ref=src,
            dst_ref=dall.at[slot, part, f],
            send_sem=d_send.at[direction],
            recv_sem=d_recv.at[direction, slot, chunk],
            device_id=(up, down)[direction],
            device_id_type=MESH,
        )

    def slot_of(direction, step):
        return step if direction == 0 else (step + 4 if not isinstance(step, int) or step < 4 else 4)

    own_d = pltpu.make_async_copy(d_ref, dall.at[0], local_sem.at[0])
    own_d.start()

    @pl.loop(0, 8)
    def _(chunk):
        for direction in (0, 1):
            d_copy(direction, None, slot_of(direction, 1), chunk).start()

    def p_copy(ring, part, k):
        slot = owner(ring, k)
        return pltpu.make_async_remote_copy(
            src_ref=pall.at[ring, part, slot],
            dst_ref=pall.at[ring, part, slot],
            send_sem=p_send.at[ring, part],
            recv_sem=p_recv.at[ring, part, k],
            device_id=targets[ring],
            device_id_type=MESH,
        )

    def sib_copy(ring, part, k):
        slot = owner(ring, k)
        return pltpu.make_async_remote_copy(
            src_ref=pall.at[ring, part, slot],
            dst_ref=pall.at[ring, part, slot],
            send_sem=sib_send,
            recv_sem=sib_recv,
            device_id=sibling,
            device_id_type=MESH,
        )

    own_p = [
        pltpu.make_async_copy(p_ref.at[part, f], pall.at[f, part, r], local_sem.at[1 + 2 * f + part])
        for f in range(F)
        for part in (0, 1)
    ]
    for copy in own_p:
        copy.start()
    for copy in own_p:
        copy.wait()

    def p_step(k):
        for part in (0, 1):
            for ring in range(F):
                p_copy(ring, part, k).start()
                sib_copy(ring, part, k).start()

    def p_wait(k):
        for part in (0, 1):
            for ring in range(F):
                p_copy(ring, part, k).wait_recv()

    def d_pass(t):
        step, chunk = 1 + t // 8, lax.rem(t, 8)
        for direction in (0, 1):
            slot = slot_of(direction, step)
            d_copy(direction, None, slot, chunk).wait_recv()
            d_copy(direction, slot, slot + 1, chunk).start()

    p_step(0)

    @pl.loop(1, NQ - 1)
    def _(k):
        for part in (0, 1):
            for ring in range(F):
                p_copy(ring, part, k - 1).wait_recv()
                p_copy(ring, part, k).start()
                sib_copy(ring, part, k).start()
        d_pass(k - 1)

    p_wait(NQ - 2)
    for part in (0, 1):
        for ring in range(F):
            sib_copy(ring, part, NQ - 1).start()
    d_pass(14)
    d_pass(15)
    own_d.wait()

    def add(slot, f, where, start=False):
        base = where * 4
        left = [
            jnp.concatenate([pall[f, part, base + i] for i in range(4)], axis=1) for part in (0, 1)
        ]
        re, im = dall[slot, 0, f], dall[slot, 1, f]
        a = jnp.dot(left[0], jnp.concatenate([re, im], axis=1), preferred_element_type=jnp.float32)
        b = jnp.dot(left[1], jnp.concatenate([im, re], axis=1), preferred_element_type=jnp.float32)
        real = a[:, :128] - b[:, :128]
        imag = a[:, 128:] + b[:, 128:]
        if start:
            o_ref[0, f] = real
            o_ref[1, f] = imag
        else:
            o_ref[0, f] += real
            o_ref[1, f] += imag

    half = pall.at[:, :, pl.ds(0, NQ)]
    whole = pltpu.make_async_remote_copy(
        src_ref=half, dst_ref=half, send_sem=sib_send, recv_sem=sib_recv, device_id=sibling, device_id_type=MESH
    )
    whole.wait_recv()

    @pl.loop(0, F)
    def _(f):
        add(0, f, z, start=True)

    def add_block(slot, where):
        @pl.loop(0, F)
        def _(f):
            add(slot, f, where)

    for step in (1, 2):
        add_block(step, lax.rem(z + NZ - step, NZ))
        add_block(step + 4, lax.rem(z + step, NZ))

    for direction in (0, 1):
        for chunk in range(8):
            pass

    def tail(chunk_pair, forward):
        for direction in (0, 1):
            slot = 3 if direction == 0 else 7
            for part in (0, 1):
                chunk = chunk_pair * 2 + part
                d_copy(direction, None, slot, chunk).wait_recv()
                if forward:
                    d_copy(direction, slot, 4, chunk).start()
        for direction in (0, 1):
            f = chunk_pair if direction == 0 else 3 - chunk_pair
            if direction == 0:
                add(3, f, lax.rem(z + NZ - 3, NZ))
            else:
                add(7, f, lax.rem(z + 3, NZ))

    @pl.loop(0, 2)
    def _(i):
        tail(i, True)

    @pl.loop(2, 4)
    def _(i):
        tail(i, False)

    @pl.loop(0, 2)
    def _(i):
        for direction in (0, 1):
            for part in (0, 1):
                d_copy(direction, None, 4, i * 2 + part).wait_recv()
            add(4, i if direction == 0 else 3 - i, lax.rem(z + 4, NZ))

    whole.wait_send()
    for ring in range(F):
        for part in (0, 1):
            ref = pall.at[ring, part, pl.ds(0, NQ - 1)]
            pltpu.make_async_remote_copy(
                src_ref=ref,
                dst_ref=ref,
                send_sem=p_send.at[ring, part],
                recv_sem=p_recv.at[ring, part, 0],
                device_id=targets[ring],
                device_id_type=MESH,
            ).wait_send()
    for direction in (0, 1):
        for ref in (dall.at[pl.ds(0, 3)], dall.at[0, :, pl.ds(0, 2)]):
            pltpu.make_async_remote_copy(
                src_ref=ref,
                dst_ref=ref,
                send_sem=d_send.at[direction],
                recv_sem=d_recv.at[direction, 1, 0],
                device_id=(up, down)[direction],
                device_id_type=MESH,
            ).wait_send()


def shards(primaries, recorded):
    return pl.pallas_call(
        kernel,
        out_shape=jax.ShapeDtypeStruct((2, F, 256, 128), jnp.float32),
        in_specs=[pl.BlockSpec(memory_space=pl.ANY)] * 2,
        out_specs=pl.BlockSpec(memory_space=pltpu.VMEM),
        scratch_shapes=[
            pltpu.VMEM((F, 2, 2 * NQ, 256, 128), jnp.bfloat16),
            pltpu.VMEM((NZ, 2, F, 512, 128), jnp.bfloat16),
            pltpu.SemaphoreType.DMA((F, 2)),
            pltpu.SemaphoreType.DMA((F, 2, NQ - 1)),
            pltpu.SemaphoreType.DMA,
            pltpu.SemaphoreType.DMA,
            pltpu.SemaphoreType.DMA((2,)),
            pltpu.SemaphoreType.DMA((2, NZ, 8)),
            pltpu.SemaphoreType.DMA((9,)),
        ],
        compiler_params=pltpu.CompilerParams(
            collective_id=0, has_side_effects=True, vmem_limit_bytes=56 * 1024 * 1024
        ),
        cost_estimate=pl.CostEstimate(flops=4294967296, bytes_accessed=3 << 20, transcendentals=0),
    )(primaries, recorded)


def solution(mesh):
    placed = (P(None, None, "shot", "rec"), P(None, None, "shot", "rec"))
    return jax.shard_map(
        shards, mesh=mesh, in_specs=placed, out_specs=P(None, None, "shot", "rec"), check_vma=False
    )
```

```python
import jax
import jax.numpy as jnp
from jax import lax
from jax.experimental import pallas as pl
from jax.experimental.pallas import tpu as pltpu
from jax.sharding import PartitionSpec as P

MESH = pl.DeviceIdType.MESH
F = 4
NZ = 8
NQ = 16
OWN12, HELP1, HELP2, OWN03 = 0, 1, 2, 3


def rec_of(x, y, c):
    return (y * 4 + x) * 2 + c


def kernel(
    p_ref, d_ref, o_ref, pall, dall, cpart, crecv,
    stage, help_send, help_recv, stage_send, stage_recv, own_send, own_recv, p_send, p_recv, sib_send, sib_recv, d_send, d_recv, c_send, c_recv, local_sem,
):
    z = lax.axis_index("shot")
    r = lax.axis_index("rec")
    c = lax.rem(r, 2)
    x = lax.rem(r // 2, 4)
    y = r // 8

    def plane(dz):
        return lax.rem(z + (dz + NZ), NZ)

    def rec(dx, dy):
        return rec_of(lax.rem(x + dx + 4, 4), lax.rem(y + dy + 4, 4), c)

    def freq(role):
        return lax.rem(z + (4 - role), 4)

    sibling = (z, rec_of(x, y, 1 - c))
    up, down, up2, down2 = ((plane(d), r) for d in (1, -1, 2, -2))
    across = (z, rec(0, 2))
    sides = ((z, rec(1, 0)), (z, rec(-1, 0))), ((z, rec(0, 1)), (z, rec(0, -1)))

    barrier = pltpu.get_barrier_semaphore()
    partners = (sibling, up, down, up2, down2, across) + sides[0] + sides[1]
    for other in partners:
        pl.semaphore_signal(barrier, inc=1, device_id=other, device_id_type=MESH)
    pl.semaphore_wait(barrier, len(partners))

    def remote(src, dst, send, recv, device):
        return pltpu.make_async_remote_copy(
            src_ref=src, dst_ref=dst, send_sem=send, recv_sem=recv, device_id=device, device_id_type=MESH
        )

    delta = lax.rem(r // 4 + NZ - z, NZ)
    delta_across = lax.rem(delta + 4, NZ)

    def is_in(values, where):
        hit = jnp.int32(0)
        for v in values:
            hit = hit + jnp.where(where == v, 1, 0)
        return hit

    AWAY = ((4, 5, 6, 7), (3, 4, 5, 6), (2, 3, 4, 5), (1, 2, 3, 4))
    HELPER = (down, down2, up2, up)
    HELP = (HELP1, HELP2, HELP2, HELP1)
    TURN = (7, 6, -1, -1)

    def moves(role, part, where):
        away = is_in(AWAY[role], where)
        turn = is_in((TURN[role],), where)
        turned = turn if part == 0 else 1 - turn
        return away * turned, away * (1 - turned)

    def help_copy(role, part, staged):
        src = stage.at[role, part] if staged else p_ref.at[part, freq(role)]
        n = 1 if staged else 0
        group = HELP[role]
        return remote(
            src, pall.at[group, part, r], help_send.at[n, role, part], help_recv.at[group, part], HELPER[role]
        )

    def stage_copy(role, part):
        return remote(
            p_ref.at[part, freq(role)], stage.at[role, part], stage_send.at[role, part], stage_recv.at[role, part], across
        )

    def own_copy(role):
        if role == 0:
            mine, dy = is_in((0, 1, 2, 3), delta), 0
        elif role == 3:
            mine, dy = is_in((0, 5, 6, 7), delta), is_in((0,), delta) * 2
        elif role == 1:
            mine, dy = is_in((7, 0, 1, 2), delta), 0
        else:
            mine = is_in((6, 7, 0, 1), delta)
            dy = is_in((7,), delta) * 3 + is_in((0,), delta) * 2 + is_in((1,), delta)
        group = OWN03 if role in (0, 3) else OWN12
        target = rec_of(x, lax.rem(y + dy, 4), c)
        src, dst = p_ref.at[:, freq(role)], pall.at[group, :, target]
        stays = mine * jnp.where(dy == 0, 1, 0)
        leaves = mine * jnp.where(dy == 0, 0, 1)

        def local():
            return pltpu.make_async_copy(src, dst, own_recv.at[group])

        def away():
            return remote(src, dst, own_send.at[role], own_recv.at[group], (z, target))

        return stays, leaves, local, away

    def when(condition, action):
        @pl.when(condition == 1)
        def _():
            action()

    def place_direct():
        for role in (3, 0, 2, 1):
            for part in (0, 1):
                when(moves(role, part, delta)[1], lambda: help_copy(role, part, False).start())

    def place_across():
        for role in (3, 0, 2, 1):
            for part in (1, 0):
                when(moves(role, part, delta)[0], lambda: stage_copy(role, part).start())

    def place_own(roles):
        for role in roles:
            stays, leaves, local, away = own_copy(role)
            when(stays, lambda: local().start())
            when(leaves, lambda: away().start())

    def place_staged():
        for role in (3, 0, 2, 1):
            for part in (1, 0):

                def pass_on():
                    stage_copy(role, part).wait_recv()
                    help_copy(role, part, True).start()

                when(moves(role, part, delta_across)[0], pass_on)

    def place_sent():
        for role in range(4):
            for part in (0, 1):
                when(moves(role, part, delta)[1], lambda: help_copy(role, part, False).wait_send())
                when(moves(role, part, delta)[0], lambda: stage_copy(role, part).wait_send())
                when(moves(role, part, delta_across)[0], lambda: help_copy(role, part, True).wait_send())
            leaves, away = own_copy(role)[1], own_copy(role)[3]
            when(leaves, lambda: away().wait_send())

    def piece_wait(group, part):
        if group in (HELP1, HELP2):
            ref = pall.at[group, part, r]
            remote(ref, ref, help_send.at[0, 0, part], help_recv.at[group, part], sibling).wait_recv()
        elif part == 0:
            ref = pall.at[group, :, r]
            pltpu.make_async_copy(ref, ref, own_recv.at[group]).wait()

    def d_copy(role, pos, part, upwards):
        f = freq(role)
        src = d_ref.at[part, f] if pos == role else dall.at[f, pos, part]
        way = 0 if upwards else 1
        return remote(src, dall.at[f, pos, part], d_send.at[way], d_recv.at[f, pos, part], up if upwards else down)

    def d_wait(role, pos):
        f = freq(role)
        for part in (0, 1):
            ref = dall.at[f, pos, part]
            remote(ref, ref, d_send.at[0], d_recv.at[f, pos, part], up).wait_recv()

    def d_forward(role, pos, upwards):
        d_wait(role, pos)
        for part in (0, 1):
            d_copy(role, pos, part, upwards).start()

    def d_own(i):
        for part in (0, 1):
            d_copy(i, i, part, True).start()
            d_copy(3 - i, 3 - i, part, False).start()

    own_d = [
        pltpu.make_async_copy(d_ref.at[:, freq(role)], dall.at[freq(role), role], local_sem.at[role]) for role in range(4)
    ]

    def slot(part, a, b):
        return rec(a, b) if part == 0 else rec(b, a)

    def p_copy(group, part, a, b, index, device, half=None):
        ref = pall.at[group, part, slot(part, a, b)]
        if half is not None:
            ref = ref.at[pl.ds(half * 128, 128)]
        return remote(ref, ref, p_send.at[group, part], p_recv.at[group, part, index], device)

    def share(group, part, a, b):
        ref = pall.at[group, part, slot(part, a, b)]
        remote(ref, ref, sib_send.at[group], sib_recv.at[group], sibling).start()

    def first(part):
        return sides[part]

    def second(part):
        return sides[1 - part]

    LINE = (0, -1, 1, 2)

    def stage1(group, parts=(0, 1)):
        for part in parts:
            piece_wait(group, part)
            for way in (0, 1):
                p_copy(group, part, 0, 0, way, first(part)[way]).start()
            for way in (0, 1):
                p_copy(group, part, 0, 0, 4 + way, second(part)[way]).start()
            share(group, part, 0, 0)

    def stage2(group):
        for way in (0, 1):
            a = LINE[1 + way]
            for part in (0, 1):
                p_copy(group, part, a, 0, way, sibling).wait_recv()
                p_copy(group, part, a, 0, 2 + way, first(part)[way], half=way).start()
                for turn in (0, 1):
                    p_copy(group, part, a, 0, 4 + 4 * (1 + way) + turn, second(part)[turn]).start()
                share(group, part, a, 0)

    def stage2b(group):
        for part in (0, 1):
            for way in (0, 1):
                p_copy(group, part, 2, 0, 2 + way, sibling, half=way).wait_recv()
            for turn in (0, 1):
                p_copy(group, part, 2, 0, 16 + turn, second(part)[turn]).start()
            share(group, part, 2, 0)

    def stage3(group):
        for i in range(4):
            for way in (0, 1):
                b = LINE[1 + way]
                for part in (0, 1):
                    p_copy(group, part, LINE[i], b, 4 + 4 * i + way, sibling).wait_recv()
                    p_copy(group, part, LINE[i], b, 6 + 4 * i + way, second(part)[way], half=way).start()
                    share(group, part, LINE[i], b)

    def stage4(group):
        for i in range(4):
            for part in (0, 1):
                for way in (0, 1):
                    p_copy(group, part, LINE[i], 2, 6 + 4 * i + way, sibling, half=way).wait_recv()
                share(group, part, LINE[i], 2)

    def shared(group):
        ref = pall.at[group, :, pl.ds(0, NQ)]
        return remote(ref, ref, sib_send.at[group], sib_recv.at[group], sibling)

    def home(group, part, role, pos):
        if group in (OWN12, OWN03):
            return plane(((0, 1, 2, 3), (-1, 0, 1, 2), (-2, -3, 4, 3), (-3, -2, -1, 4))[role][pos])
        if role == 0:
            return plane(pos if part == 0 else pos + 4)
        return plane((-3, -2, -1, 4)[pos] if part == 0 else (1, 2, 3, 0)[pos])

    def product(group, role, pos):
        f = freq(role)
        left = []
        for part in (0, 1):
            base = home(group, part, role, pos) * 4
            left.append(jnp.concatenate([pall[group, part, base + i] for i in range(4)], axis=1))
        re, im = dall[f, pos, 0], dall[f, pos, 1]
        u = jnp.dot(left[0], jnp.concatenate([re, im], axis=1), preferred_element_type=jnp.float32)
        v = jnp.dot(left[1], jnp.concatenate([im, re], axis=1), preferred_element_type=jnp.float32)
        return u[:, :128] - v[:, :128], u[:, 128:] + v[:, 128:]

    def help_with(group, role, n):
        index = (0 if role == 0 else 1) + (0 if group == HELP1 else 2)
        for part, value in enumerate(product(group, role, n if role == 0 else 3 - n)):
            if n == 0:
                cpart[index, part] = value
            else:
                cpart[index, part] += value
        if n < 3:
            return
        f = freq(role)
        near, far = (down, down2) if role == 0 else (up, up2)
        for part in (0, 1):
            remote(
                cpart.at[index, part], crecv.at[f, part], c_send.at[index], c_recv.at[f, part],
                near if group == HELP1 else far,
            ).start()

    def own_products(group, role, positions, start):
        f = freq(role)
        for n, pos in enumerate(positions):
            for part, value in enumerate(product(group, role, pos)):
                if start and n == 0:
                    o_ref[part, f] = value
                else:
                    o_ref[part, f] += value

    place_own((0, 3))
    place_direct()
    place_across()
    place_own((1, 2))
    d_own(0)
    for copy in own_d:
        copy.start()
    stage1(OWN03)
    place_staged()
    d_own(1)
    d_own(2)
    stage1(HELP1, (0,))
    stage2(OWN03)
    stage1(HELP2, (0,))
    stage1(HELP1, (1,))
    stage2(HELP1)
    stage2b(OWN03)
    stage1(HELP2, (1,))
    stage2b(HELP1)
    stage3(OWN03)
    stage2(HELP2)
    d_forward(1, 0, True)
    d_forward(2, 3, False)
    stage3(HELP1)
    stage2b(HELP2)
    d_forward(2, 1, True)
    d_forward(1, 2, False)
    stage1(OWN12)
    stage4(OWN03)
    stage3(HELP2)
    stage2(OWN12)
    stage4(HELP1)
    d_forward(2, 0, True)
    d_forward(1, 3, False)
    stage2b(OWN12)
    stage4(HELP2)
    stage3(OWN12)
    for copy in own_d:
        copy.wait()
    shared(HELP2).wait_recv()
    shared(HELP1).wait_recv()
    for n in range(4):
        if n > 0:
            d_wait(0, n)
            d_wait(3, 3 - n)
        for group in (HELP2, HELP1):
            for role in (0, 3):
                help_with(group, role, n)
    stage4(OWN12)
    shared(OWN03).wait_recv()
    own_products(OWN03, 0, (0, 1, 2, 3), True)
    own_products(OWN03, 3, (0, 1, 2, 3), True)
    shared(OWN12).wait_recv()
    own_products(OWN12, 1, (0, 1, 2, 3), True)
    own_products(OWN12, 2, (0, 1, 2, 3), True)
    for role in (0, 3, 1, 2):
        f = freq(role)
        for part in (0, 1):
            ref = crecv.at[f, part]
            remote(ref, ref, c_send.at[0], c_recv.at[f, part], up).wait_recv()
            o_ref[part, f] += crecv[f, part]

    for index in range(4):
        remote(cpart.at[index], cpart.at[index], c_send.at[index], c_recv.at[0, 0], up).wait_send()
    for group in range(4):
        shared(group).wait_send()
        for part in (0, 1):
            ref = pall.at[group, part, pl.ds(0, NQ - 1)]
            remote(ref, ref, p_send.at[group, part], p_recv.at[group, part, 0], sibling).wait_send()
    for way in (0, 1):
        ref = dall.at[pl.ds(0, 3), pl.ds(0, 2)]
        remote(ref, ref, d_send.at[way], d_recv.at[0, 0, 0], up).wait_send()
    place_sent()


def shards(primaries, recorded):
    return pl.pallas_call(
        kernel,
        out_shape=jax.ShapeDtypeStruct((2, F, 256, 128), jnp.float32),
        in_specs=[pl.BlockSpec(memory_space=pl.ANY)] * 2,
        out_specs=pl.BlockSpec(memory_space=pltpu.VMEM),
        scratch_shapes=[
            pltpu.VMEM((4, 2, 2 * NQ, 256, 128), jnp.bfloat16),
            pltpu.VMEM((F, 4, 2, 512, 128), jnp.bfloat16),
            pltpu.VMEM((4, 2, 256, 128), jnp.float32),
            pltpu.VMEM((F, 2, 256, 128), jnp.float32),
            pltpu.VMEM((4, 2, 256, 128), jnp.bfloat16),
            pltpu.SemaphoreType.DMA((2, 4, 2)),
            pltpu.SemaphoreType.DMA((4, 2)),
            pltpu.SemaphoreType.DMA((4, 2)),
            pltpu.SemaphoreType.DMA((4, 2)),
            pltpu.SemaphoreType.DMA((4,)),
            pltpu.SemaphoreType.DMA((4,)),
            pltpu.SemaphoreType.DMA((4, 2)),
            pltpu.SemaphoreType.DMA((4, 2, 20)),
            pltpu.SemaphoreType.DMA((4,)),
            pltpu.SemaphoreType.DMA((4,)),
            pltpu.SemaphoreType.DMA((2,)),
            pltpu.SemaphoreType.DMA((F, 4, 2)),
            pltpu.SemaphoreType.DMA((4,)),
            pltpu.SemaphoreType.DMA((F, 2)),
            pltpu.SemaphoreType.DMA((4,)),
        ],
        compiler_params=pltpu.CompilerParams(
            collective_id=0, has_side_effects=True, vmem_limit_bytes=56 * 1024 * 1024
        ),
        cost_estimate=pl.CostEstimate(flops=4294967296, bytes_accessed=3 << 20, transcendentals=0),
    )(primaries, recorded)


def solution(mesh):
    placed = (P(None, None, "shot", "rec"), P(None, None, "shot", "rec"))
    return jax.shard_map(
        shards, mesh=mesh, in_specs=placed, out_specs=P(None, None, "shot", "rec"), check_vma=False
    )
```

```python
import jax
import jax.numpy as jnp
from jax import lax
from jax.experimental import pallas as pl
from jax.experimental.pallas import tpu as pltpu
from jax.sharding import PartitionSpec as P

MESH = pl.DeviceIdType.MESH
F = 4
NZ = 8
NQ = 16
OWN12, HELP1, HELP2, OWN03 = 0, 1, 2, 3


def rec_of(x, y, c):
    return (y * 4 + x) * 2 + c


def kernel(
    p_ref, d_ref, o_ref, pall, dall, cpart, crecv,
    stage, help_send, help_recv, stage_send, stage_recv, own_send, own_recv, p_send, p_recv, sib_send, sib_recv, d_send, d_recv, c_send, c_recv, local_sem,
):
    z = lax.axis_index("shot")
    r = lax.axis_index("rec")
    c = lax.rem(r, 2)
    x = lax.rem(r // 2, 4)
    y = r // 8

    def plane(dz):
        return lax.rem(z + (dz + NZ), NZ)

    def rec(dx, dy):
        return rec_of(lax.rem(x + dx + 4, 4), lax.rem(y + dy + 4, 4), c)

    def freq(role):
        return lax.rem(z + (4 - role), 4)

    sibling = (z, rec_of(x, y, 1 - c))
    up, down, up2, down2 = ((plane(d), r) for d in (1, -1, 2, -2))
    across = (z, rec(0, 2))
    sides = ((z, rec(1, 0)), (z, rec(-1, 0))), ((z, rec(0, 1)), (z, rec(0, -1)))

    barrier = pltpu.get_barrier_semaphore()
    partners = (sibling, up, down, up2, down2, across) + sides[0] + sides[1]
    for other in partners:
        pl.semaphore_signal(barrier, inc=1, device_id=other, device_id_type=MESH)
    pl.semaphore_wait(barrier, len(partners))

    def remote(src, dst, send, recv, device):
        return pltpu.make_async_remote_copy(
            src_ref=src, dst_ref=dst, send_sem=send, recv_sem=recv, device_id=device, device_id_type=MESH
        )

    delta = lax.rem(r // 4 + NZ - z, NZ)
    delta_across = lax.rem(delta + 4, NZ)

    def is_in(values, where):
        hit = jnp.int32(0)
        for v in values:
            hit = hit + jnp.where(where == v, 1, 0)
        return hit

    AWAY = ((4, 5, 6, 7), (3, 4, 5, 6), (2, 3, 4, 5), (1, 2, 3, 4))
    HELPER = (down, down2, up2, up)
    HELP = (HELP1, HELP2, HELP2, HELP1)
    TURN = (7, 6, -1, -1)

    def moves(role, part, where):
        away = is_in(AWAY[role], where)
        turn = is_in((TURN[role],), where)
        turned = turn if part == 0 else 1 - turn
        return away * turned, away * (1 - turned)

    def help_copy(role, part, staged):
        src = stage.at[role, part] if staged else p_ref.at[part, freq(role)]
        n = 1 if staged else 0
        group = HELP[role]
        return remote(
            src, pall.at[group, part, r], help_send.at[n, role, part], help_recv.at[group, part], HELPER[role]
        )

    def stage_copy(role, part):
        return remote(
            p_ref.at[part, freq(role)], stage.at[role, part], stage_send.at[role, part], stage_recv.at[role, part], across
        )

    def own_copy(role):
        if role == 0:
            mine, dy = is_in((0, 1, 2, 3), delta), 0
        elif role == 3:
            mine, dy = is_in((0, 5, 6, 7), delta), is_in((0,), delta) * 2
        elif role == 1:
            mine, dy = is_in((7, 0, 1, 2), delta), 0
        else:
            mine = is_in((6, 7, 0, 1), delta)
            dy = is_in((7,), delta) * 3 + is_in((0,), delta) * 2 + is_in((1,), delta)
        group = OWN03 if role in (0, 3) else OWN12
        target = rec_of(x, lax.rem(y + dy, 4), c)
        src, dst = p_ref.at[:, freq(role)], pall.at[group, :, target]
        stays = mine * jnp.where(dy == 0, 1, 0)
        leaves = mine * jnp.where(dy == 0, 0, 1)

        def local():
            return pltpu.make_async_copy(src, dst, own_recv.at[group])

        def away():
            return remote(src, dst, own_send.at[role], own_recv.at[group], (z, target))

        return stays, leaves, local, away

    def when(condition, action):
        @pl.when(condition == 1)
        def _():
            action()

    def place_direct():
        for role in (3, 0, 2, 1):
            for part in (0, 1):
                when(moves(role, part, delta)[1], lambda: help_copy(role, part, False).start())

    def place_across():
        for role in (3, 0, 2, 1):
            for part in (1, 0):
                when(moves(role, part, delta)[0], lambda: stage_copy(role, part).start())

    def place_own(roles):
        for role in roles:
            stays, leaves, local, away = own_copy(role)
            when(stays, lambda: local().start())
            when(leaves, lambda: away().start())

    def place_staged():
        for role in (3, 0, 2, 1):
            for part in (1, 0):

                def pass_on():
                    stage_copy(role, part).wait_recv()
                    help_copy(role, part, True).start()

                when(moves(role, part, delta_across)[0], pass_on)

    def place_sent():
        for role in range(4):
            for part in (0, 1):
                when(moves(role, part, delta)[1], lambda: help_copy(role, part, False).wait_send())
                when(moves(role, part, delta)[0], lambda: stage_copy(role, part).wait_send())
                when(moves(role, part, delta_across)[0], lambda: help_copy(role, part, True).wait_send())
            leaves, away = own_copy(role)[1], own_copy(role)[3]
            when(leaves, lambda: away().wait_send())

    seen = []

    def piece_wait(group, part):
        if group in (HELP1, HELP2):
            ref = pall.at[group, part, r]
            remote(ref, ref, help_send.at[0, 0, part], help_recv.at[group, part], sibling).wait_recv()
        elif group not in seen:
            seen.append(group)
            ref = pall.at[group, :, r]
            pltpu.make_async_copy(ref, ref, own_recv.at[group]).wait()

    def d_copy(role, pos, part, upwards):
        f = freq(role)
        src = d_ref.at[part, f] if pos == role else dall.at[f, pos, part]
        way = 0 if upwards else 1
        return remote(src, dall.at[f, pos, part], d_send.at[way], d_recv.at[f, pos, part], up if upwards else down)

    def d_wait(role, pos):
        f = freq(role)
        for part in (0, 1):
            ref = dall.at[f, pos, part]
            remote(ref, ref, d_send.at[0], d_recv.at[f, pos, part], up).wait_recv()

    def d_forward(role, pos, upwards):
        d_wait(role, pos)
        for part in (0, 1):
            d_copy(role, pos, part, upwards).start()

    def d_own(i):
        for part in (0, 1):
            d_copy(i, i, part, True).start()
            d_copy(3 - i, 3 - i, part, False).start()

    own_d = [
        pltpu.make_async_copy(d_ref.at[:, freq(role)], dall.at[freq(role), role], local_sem.at[role]) for role in range(4)
    ]

    def slot(part, a, b):
        return rec(a, b) if part == 0 else rec(b, a)

    def p_copy(group, part, a, b, index, device, half=None):
        ref = pall.at[group, part, slot(part, a, b)]
        if half is not None:
            ref = ref.at[pl.ds(half * 128, 128)]
        return remote(ref, ref, p_send.at[group, part], p_recv.at[group, part, index], device)

    def share(group, part, a, b):
        ref = pall.at[group, part, slot(part, a, b)]
        remote(ref, ref, sib_send.at[group], sib_recv.at[group], sibling).start()

    def first(part):
        return sides[part]

    def second(part):
        return sides[1 - part]

    LINE = (0, -1, 1, 2)

    def stage1(group, parts=(0, 1)):
        for part in parts:
            piece_wait(group, part)
            for way in (0, 1):
                p_copy(group, part, 0, 0, way, first(part)[way]).start()
            for way in (0, 1):
                p_copy(group, part, 0, 0, 4 + way, second(part)[way]).start()
            share(group, part, 0, 0)

    def stage2(group, parts=(0, 1)):
        for way in (0, 1):
            a = LINE[1 + way]
            for part in parts:
                p_copy(group, part, a, 0, way, sibling).wait_recv()
                p_copy(group, part, a, 0, 2 + way, first(part)[way], half=way).start()
                for turn in (0, 1):
                    p_copy(group, part, a, 0, 4 + 4 * (1 + way) + turn, second(part)[turn]).start()
                share(group, part, a, 0)

    def stage2b(group, parts=(0, 1)):
        for part in parts:
            for way in (0, 1):
                p_copy(group, part, 2, 0, 2 + way, sibling, half=way).wait_recv()
            for turn in (0, 1):
                p_copy(group, part, 2, 0, 16 + turn, second(part)[turn]).start()
            share(group, part, 2, 0)

    def stage3(group, parts=(0, 1)):
        for i in range(4):
            for way in (0, 1):
                b = LINE[1 + way]
                for part in parts:
                    p_copy(group, part, LINE[i], b, 4 + 4 * i + way, sibling).wait_recv()
                    p_copy(group, part, LINE[i], b, 6 + 4 * i + way, second(part)[way], half=way).start()
                    share(group, part, LINE[i], b)

    def stage4(group, parts=(0, 1)):
        for i in range(4):
            for part in parts:
                for way in (0, 1):
                    p_copy(group, part, LINE[i], 2, 6 + 4 * i + way, sibling, half=way).wait_recv()
                share(group, part, LINE[i], 2)

    def shared(group):
        ref = pall.at[group, :, pl.ds(0, NQ)]
        return remote(ref, ref, sib_send.at[group], sib_recv.at[group], sibling)

    def home(group, part, role, pos):
        if group in (OWN12, OWN03):
            return plane(((0, 1, 2, 3), (-1, 0, 1, 2), (-2, -3, 4, 3), (-3, -2, -1, 4))[role][pos])
        if role == 0:
            return plane(pos if part == 0 else pos + 4)
        return plane((-3, -2, -1, 4)[pos] if part == 0 else (1, 2, 3, 0)[pos])

    def product(group, role, pos):
        f = freq(role)
        left = []
        for part in (0, 1):
            base = home(group, part, role, pos) * 4
            left.append(jnp.concatenate([pall[group, part, base + i] for i in range(4)], axis=1))
        re, im = dall[f, pos, 0], dall[f, pos, 1]
        u = jnp.dot(left[0], jnp.concatenate([re, im], axis=1), preferred_element_type=jnp.float32)
        v = jnp.dot(left[1], jnp.concatenate([im, re], axis=1), preferred_element_type=jnp.float32)
        return u[:, :128] - v[:, :128], u[:, 128:] + v[:, 128:]

    def help_step(group, role, n):
        index = (0 if role == 0 else 1) + (0 if group == HELP1 else 2)
        for part, value in enumerate(product(group, role, n if role == 0 else 3 - n)):
            if n == 0:
                cpart[index, part] = value
            else:
                cpart[index, part] += value

    def help_first():
        for copy in own_d:
            copy.wait()
        shared(HELP1).wait_recv()
        shared(HELP2).wait_recv()
        for n in range(3):
            if n > 0:
                d_wait(0, n)
                d_wait(3, 3 - n)
            for group in (HELP2, HELP1):
                for role in (0, 3):
                    help_step(group, role, n)

    def help_last(group):
        for role in (0, 3):
            if group == HELP2:
                d_wait(role, 3 - role)
            help_step(group, role, 3)
            index = (0 if role == 0 else 1) + (0 if group == HELP1 else 2)
            f = freq(role)
            near, far = (down, down2) if role == 0 else (up, up2)
            for part in (0, 1):
                remote(
                    cpart.at[index, part], crecv.at[f, part], c_send.at[index], c_recv.at[f, part],
                    near if group == HELP1 else far,
                ).start()

    def own_block(group):
        shared(group).wait_recv()
        for role in (0, 3) if group == OWN03 else (1, 2):
            f = freq(role)
            for pos in range(4):
                for part, value in enumerate(product(group, role, pos)):
                    if pos == 0:
                        o_ref[part, f] = value
                    else:
                        o_ref[part, f] += value

    place_across()
    place_direct()
    place_own((0, 3))
    place_own((1, 2))
    for copy in own_d:
        copy.start()
    d_own(0)
    stage1(HELP1, (0,))
    place_staged()
    stage1(HELP2, (0,))
    stage1(OWN03, (0,))
    d_own(1)
    stage2(HELP1, (0,))
    stage1(HELP1, (1,))
    d_own(2)
    stage1(HELP2, (1,))
    stage2(HELP2, (0,))
    stage2(HELP1, (1,))
    stage2b(HELP1, (0,))
    stage2(HELP2, (1,))
    d_forward(1, 0, True)
    d_forward(2, 3, False)
    stage2b(HELP2, (0,))
    stage2b(HELP1, (1,))
    d_forward(2, 1, True)
    d_forward(1, 2, False)
    stage3(HELP1, (0,))
    stage2b(HELP2, (1,))
    stage3(HELP2, (0,))
    stage3(HELP1, (1,))
    stage3(HELP2, (1,))
    stage1(OWN12, (0,))
    d_forward(2, 0, True)
    d_forward(1, 3, False)
    stage1(OWN03, (1,))
    stage4(HELP2, (0,))
    stage4(HELP1, (0,))
    stage2(OWN03, (0,))
    stage1(OWN12, (1,))
    stage4(HELP1, (1,))
    stage4(HELP2, (1,))
    stage2(OWN12, (0,))
    stage2(OWN03, (1,))
    help_first()
    stage2b(OWN03, (0,))
    stage2(OWN12, (1,))
    help_last(HELP2)
    stage2b(OWN12, (0,))
    stage2b(OWN03, (1,))
    stage2b(OWN12, (1,))
    stage3(OWN03, (0,))
    stage3(OWN03, (1,))
    stage3(OWN12, (0,))
    help_last(HELP1)
    stage3(OWN12, (1,))
    stage4(OWN03, (0,))
    stage4(OWN12, (0,))
    stage4(OWN03, (1,))
    stage4(OWN12, (1,))
    own_block(OWN03)
    own_block(OWN12)
    for role in (0, 3, 1, 2):
        f = freq(role)
        for part in (0, 1):
            ref = crecv.at[f, part]
            remote(ref, ref, c_send.at[0], c_recv.at[f, part], up).wait_recv()
            o_ref[part, f] += crecv[f, part]

    for index in range(4):
        remote(cpart.at[index], cpart.at[index], c_send.at[index], c_recv.at[0, 0], up).wait_send()
    for group in range(4):
        shared(group).wait_send()
        for part in (0, 1):
            ref = pall.at[group, part, pl.ds(0, NQ - 1)]
            remote(ref, ref, p_send.at[group, part], p_recv.at[group, part, 0], sibling).wait_send()
    for way in (0, 1):
        ref = dall.at[pl.ds(0, 3), pl.ds(0, 2)]
        remote(ref, ref, d_send.at[way], d_recv.at[0, 0, 0], up).wait_send()
    place_sent()


def shards(primaries, recorded):
    return pl.pallas_call(
        kernel,
        out_shape=jax.ShapeDtypeStruct((2, F, 256, 128), jnp.float32),
        in_specs=[pl.BlockSpec(memory_space=pl.ANY)] * 2,
        out_specs=pl.BlockSpec(memory_space=pltpu.VMEM),
        scratch_shapes=[
            pltpu.VMEM((4, 2, 2 * NQ, 256, 128), jnp.bfloat16),
            pltpu.VMEM((F, 4, 2, 512, 128), jnp.bfloat16),
            pltpu.VMEM((4, 2, 256, 128), jnp.float32),
            pltpu.VMEM((F, 2, 256, 128), jnp.float32),
            pltpu.VMEM((4, 2, 256, 128), jnp.bfloat16),
            pltpu.SemaphoreType.DMA((2, 4, 2)),
            pltpu.SemaphoreType.DMA((4, 2)),
            pltpu.SemaphoreType.DMA((4, 2)),
            pltpu.SemaphoreType.DMA((4, 2)),
            pltpu.SemaphoreType.DMA((4,)),
            pltpu.SemaphoreType.DMA((4,)),
            pltpu.SemaphoreType.DMA((4, 2)),
            pltpu.SemaphoreType.DMA((4, 2, 20)),
            pltpu.SemaphoreType.DMA((4,)),
            pltpu.SemaphoreType.DMA((4,)),
            pltpu.SemaphoreType.DMA((2,)),
            pltpu.SemaphoreType.DMA((F, 4, 2)),
            pltpu.SemaphoreType.DMA((4,)),
            pltpu.SemaphoreType.DMA((F, 2)),
            pltpu.SemaphoreType.DMA((4,)),
        ],
        compiler_params=pltpu.CompilerParams(
            collective_id=0, has_side_effects=True, vmem_limit_bytes=56 * 1024 * 1024
        ),
        cost_estimate=pl.CostEstimate(flops=4294967296, bytes_accessed=3 << 20, transcendentals=0),
    )(primaries, recorded)


def solution(mesh):
    placed = (P(None, None, "shot", "rec"), P(None, None, "shot", "rec"))
    return jax.shard_map(
        shards, mesh=mesh, in_specs=placed, out_specs=P(None, None, "shot", "rec"), check_vma=False
    )
```

```python
import jax
import jax.numpy as jnp
from jax import lax
from jax.experimental import pallas as pl
from jax.experimental.pallas import tpu as pltpu
from jax.sharding import PartitionSpec as P

MESH = pl.DeviceIdType.MESH
F = 4
NZ = 8
NQ = 16
OWN12, HELP1, HELP2, OWN03 = 0, 1, 2, 3


def rec_of(x, y, c):
    return (y * 4 + x) * 2 + c


def kernel(
    p_ref, d_ref, own_ref, other_ref, pown, pall, dall, cpart, total,
    stage, help_send, help_recv, stage_send, stage_recv, own_send, own_recv, p_send, p_recv, sib_send, sib_recv, d_send, d_recv, c_send, c_recv, local_sem,
):
    z = lax.axis_index("shot")
    r = lax.axis_index("rec")
    c = lax.rem(r, 2)
    x = lax.rem(r // 2, 4)
    y = r // 8

    def plane(dz):
        return lax.rem(z + (dz + NZ), NZ)

    def rec(dx, dy):
        return rec_of(lax.rem(x + dx + 4, 4), lax.rem(y + dy + 4, 4), c)

    def freq(role):
        return lax.rem(z + (4 - role), 4)

    sibling = (z, rec_of(x, y, 1 - c))
    up, down, up2, down2 = ((plane(d), r) for d in (1, -1, 2, -2))
    across = (z, rec(0, 2))
    sides = ((z, rec(1, 0)), (z, rec(-1, 0))), ((z, rec(0, 1)), (z, rec(0, -1)))

    own_d = [pltpu.make_async_copy(d_ref.at[:, freq(p)], dall.at[freq(p), p], local_sem.at[p]) for p in range(4)]
    own_p = pltpu.make_async_copy(p_ref, pown, local_sem.at[4])
    own_p.start()
    for copy in own_d:
        copy.start()

    barrier = pltpu.get_barrier_semaphore()
    partners = (sibling, up, down, up2, down2, across) + sides[0] + sides[1]
    for other in partners:
        pl.semaphore_signal(barrier, inc=1, device_id=other, device_id_type=MESH)
    own_p.wait()
    for copy in own_d:
        copy.wait()
    pl.semaphore_wait(barrier, len(partners))

    def remote(src, dst, send, recv, device):
        return pltpu.make_async_remote_copy(
            src_ref=src, dst_ref=dst, send_sem=send, recv_sem=recv, device_id=device, device_id_type=MESH
        )

    delta = lax.rem(r // 4 + NZ - z, NZ)
    delta_across = lax.rem(delta + 4, NZ)

    def is_in(values, where):
        hit = jnp.int32(0)
        for v in values:
            hit = hit + jnp.where(where == v, 1, 0)
        return hit

    AWAY = ((4, 5, 6, 7), (3, 4, 5, 6), (2, 3, 4, 5), (1, 2, 3, 4))
    HELPER = (down, down2, up2, up)
    HELP = (HELP1, HELP2, HELP2, HELP1)
    TURN = (7, 6, -1, -1)

    def moves(role, part, where):
        away = is_in(AWAY[role], where)
        turn = is_in((TURN[role],), where)
        turned = turn if part == 0 else 1 - turn
        return away * turned, away * (1 - turned)

    def help_copy(role, part, staged):
        src = stage.at[role, part] if staged else pown.at[part, freq(role)]
        n = 1 if staged else 0
        group = HELP[role]
        return remote(
            src, pall.at[group, part, r], help_send.at[n, role, part], help_recv.at[group, part], HELPER[role]
        )

    def stage_copy(role, part):
        return remote(
            pown.at[part, freq(role)], stage.at[role, part], stage_send.at[role, part], stage_recv.at[role, part], across
        )

    def own_copy(role):
        if role == 0:
            mine, dy = is_in((0, 1, 2, 3), delta), 0
        elif role == 3:
            mine, dy = is_in((0, 5, 6, 7), delta), is_in((0,), delta) * 2
        elif role == 1:
            mine, dy = is_in((7, 0, 1, 2), delta), 0
        else:
            mine = is_in((6, 7, 0, 1), delta)
            dy = is_in((7,), delta) * 3 + is_in((0,), delta) * 2 + is_in((1,), delta)
        group = OWN03 if role in (0, 3) else OWN12
        target = rec_of(x, lax.rem(y + dy, 4), c)
        src, dst = pown.at[:, freq(role)], pall.at[group, :, target]
        stays = mine * jnp.where(dy == 0, 1, 0)
        leaves = mine * jnp.where(dy == 0, 0, 1)

        def local():
            return pltpu.make_async_copy(src, dst, own_recv.at[group])

        def away():
            return remote(src, dst, own_send.at[role], own_recv.at[group], (z, target))

        return stays, leaves, local, away

    def when(condition, action):
        @pl.when(condition == 1)
        def _():
            action()

    def place_direct():
        for role in (3, 0, 2, 1):
            for part in (0, 1):
                when(moves(role, part, delta)[1], lambda: help_copy(role, part, False).start())

    def place_across():
        for role in (3, 0, 2, 1):
            for part in (1, 0):
                when(moves(role, part, delta)[0], lambda: stage_copy(role, part).start())

    def place_own(roles):
        for role in roles:
            stays, leaves, local, away = own_copy(role)
            when(stays, lambda: local().start())
            when(leaves, lambda: away().start())

    def place_staged():
        for role in (3, 0, 2, 1):
            for part in (1, 0):

                def pass_on():
                    stage_copy(role, part).wait_recv()
                    help_copy(role, part, True).start()

                when(moves(role, part, delta_across)[0], pass_on)

    def place_sent():
        for role in range(4):
            for part in (0, 1):
                when(moves(role, part, delta)[1], lambda: help_copy(role, part, False).wait_send())
                when(moves(role, part, delta)[0], lambda: stage_copy(role, part).wait_send())
                when(moves(role, part, delta_across)[0], lambda: help_copy(role, part, True).wait_send())
            leaves, away = own_copy(role)[1], own_copy(role)[3]
            when(leaves, lambda: away().wait_send())

    seen = []

    def piece_wait(group, part):
        if group in (HELP1, HELP2):
            ref = pall.at[group, part, r]
            remote(ref, ref, help_send.at[0, 0, part], help_recv.at[group, part], sibling).wait_recv()
        elif group not in seen:
            seen.append(group)
            ref = pall.at[group, :, r]
            pltpu.make_async_copy(ref, ref, own_recv.at[group]).wait()

    def d_copy(role, pos, part, upwards):
        f = freq(role)
        src = dall.at[f, pos, part]
        way = 0 if upwards else 1
        return remote(src, dall.at[f, pos, part], d_send.at[way], d_recv.at[f, pos, part], up if upwards else down)

    def d_wait(role, pos):
        f = freq(role)
        for part in (0, 1):
            ref = dall.at[f, pos, part]
            remote(ref, ref, d_send.at[0], d_recv.at[f, pos, part], up).wait_recv()

    def d_forward(role, pos, upwards):
        d_wait(role, pos)
        for part in (0, 1):
            d_copy(role, pos, part, upwards).start()

    def d_own(i):
        for part in (0, 1):
            d_copy(i, i, part, True).start()
            d_copy(3 - i, 3 - i, part, False).start()

    def slot(part, a, b):
        return rec(a, b) if part == 0 else rec(b, a)

    def p_copy(group, part, a, b, index, device, half=None):
        ref = pall.at[group, part, slot(part, a, b)]
        if half is not None:
            ref = ref.at[pl.ds(half * 128, 128)]
        return remote(ref, ref, p_send.at[group, part], p_recv.at[group, part, index], device)

    def share(group, part, a, b):
        ref = pall.at[group, part, slot(part, a, b)]
        remote(ref, ref, sib_send.at[group], sib_recv.at[group], sibling).start()

    def first(part):
        return sides[part]

    def second(part):
        return sides[1 - part]

    LINE = (0, -1, 1, 2)

    def stage1(group, parts=(0, 1)):
        for part in parts:
            piece_wait(group, part)
            for way in (0, 1):
                p_copy(group, part, 0, 0, way, first(part)[way]).start()
            for way in (0, 1):
                p_copy(group, part, 0, 0, 4 + way, second(part)[way]).start()
            share(group, part, 0, 0)

    def stage2(group, parts=(0, 1)):
        for way in (0, 1):
            a = LINE[1 + way]
            for part in parts:
                p_copy(group, part, a, 0, way, sibling).wait_recv()
                p_copy(group, part, a, 0, 2 + way, first(part)[way], half=way).start()
                for turn in (0, 1):
                    p_copy(group, part, a, 0, 4 + 4 * (1 + way) + turn, second(part)[turn]).start()
                share(group, part, a, 0)

    def stage2b(group, parts=(0, 1)):
        for part in parts:
            for way in (0, 1):
                p_copy(group, part, 2, 0, 2 + way, sibling, half=way).wait_recv()
            for turn in (0, 1):
                p_copy(group, part, 2, 0, 16 + turn, second(part)[turn]).start()
            share(group, part, 2, 0)

    def stage3(group, parts=(0, 1)):
        for i in range(4):
            for way in (0, 1):
                b = LINE[1 + way]
                for part in parts:
                    p_copy(group, part, LINE[i], b, 4 + 4 * i + way, sibling).wait_recv()
                    p_copy(group, part, LINE[i], b, 6 + 4 * i + way, second(part)[way], half=way).start()
                    share(group, part, LINE[i], b)

    def stage4(group, parts=(0, 1)):
        for i in range(4):
            for part in parts:
                for way in (0, 1):
                    p_copy(group, part, LINE[i], 2, 6 + 4 * i + way, sibling, half=way).wait_recv()
                share(group, part, LINE[i], 2)

    def shared(group):
        ref = pall.at[group, :, pl.ds(0, NQ)]
        return remote(ref, ref, sib_send.at[group], sib_recv.at[group], sibling)

    def home(group, part, role, pos):
        if group in (OWN12, OWN03):
            return plane(((0, 1, 2, 3), (-1, 0, 1, 2), (-2, -3, 4, 3), (-3, -2, -1, 4))[role][pos])
        if role == 0:
            return plane(pos if part == 0 else pos + 4)
        return plane((-3, -2, -1, 4)[pos] if part == 0 else (1, 2, 3, 0)[pos])

    def product(group, role, pos):
        f = freq(role)
        left = []
        for part in (0, 1):
            base = home(group, part, role, pos) * 4
            left.append(jnp.concatenate([pall[group, part, base + i] for i in range(4)], axis=1))
        re, im = dall[f, pos, 0], dall[f, pos, 1]
        u = jnp.dot(left[0], jnp.concatenate([re, im], axis=1), preferred_element_type=jnp.float32)
        v = jnp.dot(left[1], jnp.concatenate([im, re], axis=1), preferred_element_type=jnp.float32)
        return u[:, :128] - v[:, :128], u[:, 128:] + v[:, 128:]

    def help_step(group, role, n):
        index = (0 if role == 0 else 1) + (0 if group == HELP1 else 2)
        for part, value in enumerate(product(group, role, n if role == 0 else 3 - n)):
            if n == 0:
                cpart[index, part] = value
            else:
                cpart[index, part] += value

    waited = []

    def d_once(role, pos):
        if (role, pos) not in waited:
            waited.append((role, pos))
            d_wait(role, pos)

    def help_first(group, n):
        if n == 0:
            shared(group).wait_recv()
        for role in (0, 3):
            if n > 0:
                d_once(role, n if role == 0 else 3 - n)
            help_step(group, role, n)

    def help_last(group):
        for role in (0, 3):
            d_once(role, 3 - role)
            help_step(group, role, 3)
            index = (0 if role == 0 else 1) + (0 if group == HELP1 else 2)
            f = freq(role)
            near, far = (down, down2) if role == 0 else (up, up2)
            for part in (0, 1):
                remote(
                    cpart.at[index, part], other_ref.at[part, f], c_send.at[index], c_recv.at[f, part],
                    near if group == HELP1 else far,
                ).start()

    def out_copy(role):
        f = freq(role)
        return pltpu.make_async_copy(total.at[:, f], own_ref.at[:, f], local_sem.at[role])

    def own_block(group):
        shared(group).wait_recv()
        for role in (0, 3) if group == OWN03 else (1, 2):
            f = freq(role)
            for pos in range(4):
                for part, value in enumerate(product(group, role, pos)):
                    if pos == 0:
                        total[part, f] = value
                    else:
                        total[part, f] += value
            out_copy(role).start()

    place_across()
    place_direct()
    place_own((0, 3))
    place_own((1, 2))
    d_own(0)
    stage1(OWN03, (1,))
    stage1(HELP1, (0,))
    place_staged()
    d_own(1)
    stage1(HELP2, (0,))
    stage1(OWN12, (0,))
    stage1(OWN03, (0,))
    stage1(HELP1, (1,))
    stage1(HELP2, (1,))
    d_own(2)
    stage2(HELP2, (0,))
    d_forward(1, 0, True)
    d_forward(2, 3, False)
    stage2(HELP1, (1,))
    stage2(HELP2, (1,))
    stage2b(HELP2, (0,))
    d_forward(2, 1, True)
    d_forward(1, 2, False)
    stage2(HELP1, (0,))
    stage2b(HELP2, (1,))
    stage3(HELP2, (0,))
    stage2b(HELP1, (1,))
    stage2b(HELP1, (0,))
    stage3(HELP2, (1,))
    stage3(HELP1, (1,))
    stage2(OWN03, (1,))
    d_forward(2, 0, True)
    d_forward(1, 3, False)
    stage3(HELP1, (0,))
    stage4(HELP2, (1,))
    stage1(OWN12, (1,))
    stage2(OWN03, (0,))
    stage4(HELP2, (0,))
    stage4(HELP1, (1,))
    stage4(HELP1, (0,))
    stage2b(OWN03, (1,))
    help_first(HELP2, 0)
    help_first(HELP2, 1)
    help_first(HELP1, 0)
    stage2(OWN12, (0,))
    help_first(HELP1, 1)
    help_first(HELP1, 2)
    help_first(HELP2, 2)
    stage2(OWN12, (1,))
    help_last(HELP2)
    help_last(HELP1)
    stage2b(OWN03, (0,))
    stage2b(OWN12, (0,))
    stage3(OWN03, (1,))
    stage3(OWN03, (0,))
    stage2b(OWN12, (1,))
    stage3(OWN12, (0,))
    stage3(OWN12, (1,))
    stage4(OWN03, (1,))
    stage4(OWN03, (0,))
    stage4(OWN12, (0,))
    stage4(OWN12, (1,))
    own_block(OWN03)
    own_block(OWN12)
    for role in (0, 3, 1, 2):
        f = freq(role)
        out_copy(role).wait()
        for part in (0, 1):
            ref = other_ref.at[part, f]
            remote(ref, ref, c_send.at[0], c_recv.at[f, part], up).wait_recv()

    for index in range(4):
        remote(cpart.at[index], cpart.at[index], c_send.at[index], c_recv.at[0, 0], up).wait_send()
    for group in range(4):
        shared(group).wait_send()
        for part in (0, 1):
            ref = pall.at[group, part, pl.ds(0, NQ - 1)]
            remote(ref, ref, p_send.at[group, part], p_recv.at[group, part, 0], sibling).wait_send()
    for way in (0, 1):
        ref = dall.at[pl.ds(0, 3), pl.ds(0, 2)]
        remote(ref, ref, d_send.at[way], d_recv.at[0, 0, 0], up).wait_send()
    place_sent()


def shards(primaries, recorded):
    own, other = pl.pallas_call(
        kernel,
        out_shape=(jax.ShapeDtypeStruct((2, F, 256, 128), jnp.float32),) * 2,
        in_specs=[pl.BlockSpec(memory_space=pl.ANY)] * 2,
        out_specs=(pl.BlockSpec(memory_space=pl.ANY),) * 2,
        scratch_shapes=[
            pltpu.VMEM((2, F, 256, 128), jnp.bfloat16),
            pltpu.VMEM((4, 2, 2 * NQ, 256, 128), jnp.bfloat16),
            pltpu.VMEM((F, 4, 2, 512, 128), jnp.bfloat16),
            pltpu.VMEM((4, 2, 256, 128), jnp.float32),
            pltpu.VMEM((2, F, 256, 128), jnp.float32),
            pltpu.VMEM((4, 2, 256, 128), jnp.bfloat16),
            pltpu.SemaphoreType.DMA((2, 4, 2)),
            pltpu.SemaphoreType.DMA((4, 2)),
            pltpu.SemaphoreType.DMA((4, 2)),
            pltpu.SemaphoreType.DMA((4, 2)),
            pltpu.SemaphoreType.DMA((4,)),
            pltpu.SemaphoreType.DMA((4,)),
            pltpu.SemaphoreType.DMA((4, 2)),
            pltpu.SemaphoreType.DMA((4, 2, 20)),
            pltpu.SemaphoreType.DMA((4,)),
            pltpu.SemaphoreType.DMA((4,)),
            pltpu.SemaphoreType.DMA((2,)),
            pltpu.SemaphoreType.DMA((F, 4, 2)),
            pltpu.SemaphoreType.DMA((4,)),
            pltpu.SemaphoreType.DMA((F, 2)),
            pltpu.SemaphoreType.DMA((5,)),
        ],
        compiler_params=pltpu.CompilerParams(
            collective_id=0, has_side_effects=True, vmem_limit_bytes=56 * 1024 * 1024
        ),
        cost_estimate=pl.CostEstimate(flops=4294967296, bytes_accessed=3 << 20, transcendentals=0),
    )(primaries, recorded)
    return own + other


def solution(mesh):
    placed = (P(None, None, "shot", "rec"), P(None, None, "shot", "rec"))
    return jax.shard_map(
        shards, mesh=mesh, in_specs=placed, out_specs=P(None, None, "shot", "rec"), check_vma=False
    )
```

```python
import jax
import jax.numpy as jnp
from jax import lax
from jax.experimental import pallas as pl
from jax.experimental.pallas import tpu as pltpu
from jax.sharding import PartitionSpec as P

MESH = pl.DeviceIdType.MESH
F = 4
NZ = 8
NQ = 16
OWN12, HELP1, HELP2, OWN03 = 0, 1, 2, 3


def rec_of(x, y, c):
    return (y * 4 + x) * 2 + c


def kernel(
    p_ref, d_ref, own_ref, other_ref, pown, pall, dall, cpart, total,
    stage, help_send, help_recv, stage_send, stage_recv, own_send, own_recv, p_send, p_recv, sib_send, sib_recv, d_send, d_recv, c_send, c_recv, local_sem,
):
    z = lax.axis_index("shot")
    r = lax.axis_index("rec")
    c = lax.rem(r, 2)
    x = lax.rem(r // 2, 4)
    y = r // 8

    def plane(dz):
        return lax.rem(z + (dz + NZ), NZ)

    def rec(dx, dy):
        return rec_of(lax.rem(x + dx + 4, 4), lax.rem(y + dy + 4, 4), c)

    def freq(role):
        return lax.rem(z + (4 - role), 4)

    sibling = (z, rec_of(x, y, 1 - c))
    up, down, up2, down2 = ((plane(d), r) for d in (1, -1, 2, -2))
    across = (z, rec(0, 2))
    sides = ((z, rec(1, 0)), (z, rec(-1, 0))), ((z, rec(0, 1)), (z, rec(0, -1)))

    own_d = [pltpu.make_async_copy(d_ref.at[:, freq(p)], dall.at[freq(p), p], local_sem.at[p]) for p in range(4)]
    own_p = pltpu.make_async_copy(p_ref, pown, local_sem.at[4])
    own_p.start()
    for copy in own_d:
        copy.start()

    barrier = pltpu.get_barrier_semaphore()
    partners = (sibling, up, down, up2, down2, across) + sides[0] + sides[1]
    for other in partners:
        pl.semaphore_signal(barrier, inc=1, device_id=other, device_id_type=MESH)
    own_p.wait()
    for copy in own_d:
        copy.wait()
    pl.semaphore_wait(barrier, len(partners))

    def remote(src, dst, send, recv, device):
        return pltpu.make_async_remote_copy(
            src_ref=src, dst_ref=dst, send_sem=send, recv_sem=recv, device_id=device, device_id_type=MESH
        )

    delta = lax.rem(r // 4 + NZ - z, NZ)
    delta_across = lax.rem(delta + 4, NZ)

    def is_in(values, where):
        hit = jnp.int32(0)
        for v in values:
            hit = hit + jnp.where(where == v, 1, 0)
        return hit

    AWAY = ((4, 5, 6, 7), (3, 4, 5, 6), (2, 3, 4, 5), (1, 2, 3, 4))
    HELPER = (down, down2, up2, up)
    HELP = (HELP1, HELP2, HELP2, HELP1)
    TURN = (7, 6, -1, -1)

    def moves(role, part, where):
        away = is_in(AWAY[role], where)
        turn = is_in((TURN[role],), where)
        turned = turn if part == 0 else 1 - turn
        return away * turned, away * (1 - turned)

    def help_copy(role, part, staged):
        src = stage.at[role, part] if staged else pown.at[part, freq(role)]
        n = 1 if staged else 0
        group = HELP[role]
        return remote(
            src, pall.at[group, part, r], help_send.at[n, role, part], help_recv.at[group, part], HELPER[role]
        )

    def stage_copy(role, part):
        return remote(
            pown.at[part, freq(role)], stage.at[role, part], stage_send.at[role, part], stage_recv.at[role, part], across
        )

    def own_copy(role):
        if role == 0:
            mine, dy = is_in((0, 1, 2, 3), delta), 0
        elif role == 3:
            mine, dy = is_in((0, 5, 6, 7), delta), is_in((0,), delta) * 2
        elif role == 1:
            mine, dy = is_in((7, 0, 1, 2), delta), 0
        else:
            mine = is_in((6, 7, 0, 1), delta)
            dy = is_in((7,), delta) * 3 + is_in((0,), delta) * 2 + is_in((1,), delta)
        group = OWN03 if role in (0, 3) else OWN12
        target = rec_of(x, lax.rem(y + dy, 4), c)
        src, dst = pown.at[:, freq(role)], pall.at[group, :, target]
        stays = mine * jnp.where(dy == 0, 1, 0)
        leaves = mine * jnp.where(dy == 0, 0, 1)

        def local():
            return pltpu.make_async_copy(src, dst, own_recv.at[group])

        def away():
            return remote(src, dst, own_send.at[role], own_recv.at[group], (z, target))

        return stays, leaves, local, away

    def when(condition, action):
        @pl.when(condition == 1)
        def _():
            action()

    def place_direct():
        for role in (3, 0, 2, 1):
            for part in (0, 1):
                when(moves(role, part, delta)[1], lambda: help_copy(role, part, False).start())

    def place_across():
        for role in (3, 0, 2, 1):
            for part in (1, 0):
                when(moves(role, part, delta)[0], lambda: stage_copy(role, part).start())

    def place_own(roles):
        for role in roles:
            stays, leaves, local, away = own_copy(role)
            when(stays, lambda: local().start())
            when(leaves, lambda: away().start())

    def place_staged():
        for role in (3, 0, 2, 1):
            for part in (1, 0):

                def pass_on():
                    stage_copy(role, part).wait_recv()
                    help_copy(role, part, True).start()

                when(moves(role, part, delta_across)[0], pass_on)

    def place_sent():
        for role in range(4):
            for part in (0, 1):
                when(moves(role, part, delta)[1], lambda: help_copy(role, part, False).wait_send())
                when(moves(role, part, delta)[0], lambda: stage_copy(role, part).wait_send())
                when(moves(role, part, delta_across)[0], lambda: help_copy(role, part, True).wait_send())
            leaves, away = own_copy(role)[1], own_copy(role)[3]
            when(leaves, lambda: away().wait_send())

    seen = []

    def piece_wait(group, part):
        if group in (HELP1, HELP2):
            ref = pall.at[group, part, r]
            remote(ref, ref, help_send.at[0, 0, part], help_recv.at[group, part], sibling).wait_recv()
        elif group not in seen:
            seen.append(group)
            ref = pall.at[group, :, r]
            pltpu.make_async_copy(ref, ref, own_recv.at[group]).wait()

    def d_copy(role, pos, part, upwards):
        f = freq(role)
        src = dall.at[f, pos, part]
        way = 0 if upwards else 1
        return remote(src, dall.at[f, pos, part], d_send.at[way], d_recv.at[f, pos, part], up if upwards else down)

    def d_wait(role, pos):
        f = freq(role)
        for part in (0, 1):
            ref = dall.at[f, pos, part]
            remote(ref, ref, d_send.at[0], d_recv.at[f, pos, part], up).wait_recv()

    def d_forward(role, pos, upwards):
        d_wait(role, pos)
        for part in (0, 1):
            d_copy(role, pos, part, upwards).start()

    def d_own(i):
        for part in (0, 1):
            d_copy(i, i, part, True).start()
            d_copy(3 - i, 3 - i, part, False).start()

    def slot(part, a, b):
        return rec(a, b) if part == 0 else rec(b, a)

    def p_copy(group, part, a, b, index, device, half=None):
        ref = pall.at[group, part, slot(part, a, b)]
        if half is not None:
            ref = ref.at[pl.ds(half * 128, 128)]
        return remote(ref, ref, p_send.at[group, part], p_recv.at[group, part, index], device)

    def share(group, part, a, b):
        ref = pall.at[group, part, slot(part, a, b)]
        remote(ref, ref, sib_send.at[group], sib_recv.at[group], sibling).start()

    def first(part):
        return sides[part]

    def second(part):
        return sides[1 - part]

    LINE = (0, -1, 1, 2)

    def stage1(group, parts=(0, 1)):
        for part in parts:
            piece_wait(group, part)
            for way in (0, 1):
                p_copy(group, part, 0, 0, way, first(part)[way]).start()
            for way in (0, 1):
                p_copy(group, part, 0, 0, 4 + way, second(part)[way]).start()
            share(group, part, 0, 0)

    def stage2(group, parts=(0, 1)):
        for way in (0, 1):
            a = LINE[1 + way]
            for part in parts:
                p_copy(group, part, a, 0, way, sibling).wait_recv()
                p_copy(group, part, a, 0, 2 + way, first(part)[way], half=way).start()
                for turn in (0, 1):
                    p_copy(group, part, a, 0, 4 + 4 * (1 + way) + turn, second(part)[turn]).start()
                share(group, part, a, 0)

    def stage2b(group, parts=(0, 1)):
        for part in parts:
            for way in (0, 1):
                p_copy(group, part, 2, 0, 2 + way, sibling, half=way).wait_recv()
            for turn in (0, 1):
                p_copy(group, part, 2, 0, 16 + turn, second(part)[turn]).start()
            share(group, part, 2, 0)

    def stage3(group, parts=(0, 1)):
        for i in range(4):
            for way in (0, 1):
                b = LINE[1 + way]
                for part in parts:
                    p_copy(group, part, LINE[i], b, 4 + 4 * i + way, sibling).wait_recv()
                    p_copy(group, part, LINE[i], b, 6 + 4 * i + way, second(part)[way], half=way).start()
                    share(group, part, LINE[i], b)

    def stage4(group, parts=(0, 1)):
        for i in range(4):
            for part in parts:
                for way in (0, 1):
                    p_copy(group, part, LINE[i], 2, 6 + 4 * i + way, sibling, half=way).wait_recv()
                share(group, part, LINE[i], 2)

    def shared(group):
        ref = pall.at[group, :, pl.ds(0, NQ)]
        return remote(ref, ref, sib_send.at[group], sib_recv.at[group], sibling)

    def home(group, part, role, pos):
        if group in (OWN12, OWN03):
            return plane(((0, 1, 2, 3), (-1, 0, 1, 2), (-2, -3, 4, 3), (-3, -2, -1, 4))[role][pos])
        if role == 0:
            return plane(pos if part == 0 else pos + 4)
        return plane((-3, -2, -1, 4)[pos] if part == 0 else (1, 2, 3, 0)[pos])

    def product(group, role, pos):
        f = freq(role)
        left = []
        for part in (0, 1):
            base = home(group, part, role, pos) * 4
            left.append(jnp.concatenate([pall[group, part, base + i] for i in range(4)], axis=1))
        re, im = dall[f, pos, 0], dall[f, pos, 1]
        u = jnp.dot(left[0], jnp.concatenate([re, im], axis=1), preferred_element_type=jnp.float32)
        v = jnp.dot(left[1], jnp.concatenate([im, re], axis=1), preferred_element_type=jnp.float32)
        return u[:, :128] - v[:, :128], u[:, 128:] + v[:, 128:]

    def help_step(group, role, n):
        index = (0 if role == 0 else 1) + (0 if group == HELP1 else 2)
        for part, value in enumerate(product(group, role, n if role == 0 else 3 - n)):
            if n == 0:
                cpart[index, part] = value
            else:
                cpart[index, part] += value

    waited = []

    def d_once(role, pos):
        if (role, pos) not in waited:
            waited.append((role, pos))
            d_wait(role, pos)

    def help_first(group, n):
        if n == 0:
            shared(group).wait_recv()
        for role in (0, 3):
            if n > 0:
                d_once(role, n if role == 0 else 3 - n)
            help_step(group, role, n)

    def help_last(group):
        for role in (0, 3):
            d_once(role, 3 - role)
            help_step(group, role, 3)
            index = (0 if role == 0 else 1) + (0 if group == HELP1 else 2)
            f = freq(role)
            near, far = (down, down2) if role == 0 else (up, up2)
            for part in (0, 1):
                remote(
                    cpart.at[index, part], other_ref.at[part, f], c_send.at[index], c_recv.at[f, part],
                    near if group == HELP1 else far,
                ).start()

    def out_copy(role):
        f = freq(role)
        return pltpu.make_async_copy(total.at[:, f], own_ref.at[:, f], local_sem.at[role])

    def own_block(group):
        shared(group).wait_recv()
        for role in (0, 3) if group == OWN03 else (1, 2):
            f = freq(role)
            for pos in range(4):
                for part, value in enumerate(product(group, role, pos)):
                    if pos == 0:
                        total[part, f] = value
                    else:
                        total[part, f] += value
            out_copy(role).start()

    place_across()
    place_direct()
    place_own((0, 3))
    place_own((1, 2))
    d_own(0)
    stage1(OWN03, (1,))
    stage1(HELP1, (0,))
    place_staged()
    stage1(OWN03, (0,))
    stage1(OWN12, (1,))
    stage1(HELP2, (0,))
    d_own(1)
    d_own(2)
    d_forward(1, 0, True)
    d_forward(2, 3, False)
    stage1(HELP1, (1,))
    stage1(HELP2, (1,))
    stage2(HELP2, (0,))
    stage2(HELP1, (1,))
    stage2(HELP2, (1,))
    stage2b(HELP2, (0,))
    stage2(HELP1, (0,))
    stage2b(HELP2, (1,))
    d_forward(2, 1, True)
    d_forward(1, 2, False)
    stage2b(HELP1, (1,))
    stage3(HELP2, (0,))
    stage2b(HELP1, (0,))
    stage3(HELP2, (1,))
    stage3(HELP1, (1,))
    stage3(HELP1, (0,))
    d_forward(2, 0, True)
    d_forward(1, 3, False)
    stage2(OWN03, (0,))
    stage2(OWN03, (1,))
    stage4(HELP2, (0,))
    stage4(HELP2, (1,))
    stage4(HELP1, (1,))
    stage4(HELP1, (0,))
    stage2b(OWN03, (0,))
    stage1(OWN12, (0,))
    help_first(HELP2, 0)
    help_first(HELP2, 1)
    stage2(OWN12, (1,))
    help_first(HELP2, 2)
    stage3(OWN03, (0,))
    stage2b(OWN03, (1,))
    stage2(OWN12, (0,))
    help_last(HELP2)
    help_first(HELP1, 0)
    help_first(HELP1, 1)
    help_first(HELP1, 2)
    help_last(HELP1)
    stage2b(OWN12, (1,))
    stage3(OWN03, (1,))
    stage2b(OWN12, (0,))
    stage3(OWN12, (1,))
    stage3(OWN12, (0,))
    stage4(OWN03, (1,))
    stage4(OWN03, (0,))
    stage4(OWN12, (1,))
    stage4(OWN12, (0,))
    own_block(OWN03)
    own_block(OWN12)
    for role in (0, 3, 1, 2):
        f = freq(role)
        out_copy(role).wait()
        for part in (0, 1):
            ref = other_ref.at[part, f]
            remote(ref, ref, c_send.at[0], c_recv.at[f, part], up).wait_recv()

    for index in range(4):
        remote(cpart.at[index], cpart.at[index], c_send.at[index], c_recv.at[0, 0], up).wait_send()
    for group in range(4):
        shared(group).wait_send()
        for part in (0, 1):
            ref = pall.at[group, part, pl.ds(0, NQ - 1)]
            remote(ref, ref, p_send.at[group, part], p_recv.at[group, part, 0], sibling).wait_send()
    for way in (0, 1):
        ref = dall.at[pl.ds(0, 3), pl.ds(0, 2)]
        remote(ref, ref, d_send.at[way], d_recv.at[0, 0, 0], up).wait_send()
    place_sent()


def shards(primaries, recorded):
    own, other = pl.pallas_call(
        kernel,
        out_shape=(jax.ShapeDtypeStruct((2, F, 256, 128), jnp.float32),) * 2,
        in_specs=[pl.BlockSpec(memory_space=pl.ANY)] * 2,
        out_specs=(pl.BlockSpec(memory_space=pl.ANY),) * 2,
        scratch_shapes=[
            pltpu.VMEM((2, F, 256, 128), jnp.bfloat16),
            pltpu.VMEM((4, 2, 2 * NQ, 256, 128), jnp.bfloat16),
            pltpu.VMEM((F, 4, 2, 512, 128), jnp.bfloat16),
            pltpu.VMEM((4, 2, 256, 128), jnp.float32),
            pltpu.VMEM((2, F, 256, 128), jnp.float32),
            pltpu.VMEM((4, 2, 256, 128), jnp.bfloat16),
            pltpu.SemaphoreType.DMA((2, 4, 2)),
            pltpu.SemaphoreType.DMA((4, 2)),
            pltpu.SemaphoreType.DMA((4, 2)),
            pltpu.SemaphoreType.DMA((4, 2)),
            pltpu.SemaphoreType.DMA((4,)),
            pltpu.SemaphoreType.DMA((4,)),
            pltpu.SemaphoreType.DMA((4, 2)),
            pltpu.SemaphoreType.DMA((4, 2, 20)),
            pltpu.SemaphoreType.DMA((4,)),
            pltpu.SemaphoreType.DMA((4,)),
            pltpu.SemaphoreType.DMA((2,)),
            pltpu.SemaphoreType.DMA((F, 4, 2)),
            pltpu.SemaphoreType.DMA((4,)),
            pltpu.SemaphoreType.DMA((F, 2)),
            pltpu.SemaphoreType.DMA((5,)),
        ],
        compiler_params=pltpu.CompilerParams(
            collective_id=0, has_side_effects=True, vmem_limit_bytes=56 * 1024 * 1024
        ),
        cost_estimate=pl.CostEstimate(flops=4294967296, bytes_accessed=3 << 20, transcendentals=0),
    )(primaries, recorded)
    return own + other


def solution(mesh):
    placed = (P(None, None, "shot", "rec"), P(None, None, "shot", "rec"))
    return jax.shard_map(
        shards, mesh=mesh, in_specs=placed, out_specs=P(None, None, "shot", "rec"), check_vma=False
    )
```

```python
import jax
import jax.numpy as jnp
from jax import lax
from jax.experimental import pallas as pl
from jax.experimental.pallas import tpu as pltpu
from jax.sharding import PartitionSpec as P

MESH = pl.DeviceIdType.MESH
F = 4
NZ = 8
NQ = 16
OWN12, HELP1, HELP2, OWN03 = 0, 1, 2, 3


def rec_of(x, y, c):
    return (y * 4 + x) * 2 + c


def kernel(
    p_ref, d_ref, own_ref, other_ref, pown, pall, dall, cpart, total,
    stage, help_send, help_recv, stage_send, stage_recv, own_send, own_recv, p_send, p_recv, sib_send, sib_recv, d_send, d_recv, c_send, c_recv, local_sem,
):
    z = lax.axis_index("shot")
    r = lax.axis_index("rec")
    c = lax.rem(r, 2)
    x = lax.rem(r // 2, 4)
    y = r // 8

    def plane(dz):
        return lax.rem(z + (dz + NZ), NZ)

    def rec(dx, dy):
        return rec_of(lax.rem(x + dx + 4, 4), lax.rem(y + dy + 4, 4), c)

    def freq(role):
        return lax.rem(z + (4 - role), 4)

    sibling = (z, rec_of(x, y, 1 - c))
    up, down, up2, down2 = ((plane(d), r) for d in (1, -1, 2, -2))
    across = (z, rec(0, 2))
    sides = ((z, rec(1, 0)), (z, rec(-1, 0))), ((z, rec(0, 1)), (z, rec(0, -1)))

    own_d = [pltpu.make_async_copy(d_ref.at[:, freq(p)], dall.at[freq(p), p], local_sem.at[p]) for p in range(4)]
    own_p = pltpu.make_async_copy(p_ref, pown, local_sem.at[4])
    own_p.start()
    for copy in own_d:
        copy.start()

    barrier = pltpu.get_barrier_semaphore()
    partners = (sibling, up, down, up2, down2, across) + sides[0] + sides[1]
    for other in partners:
        pl.semaphore_signal(barrier, inc=1, device_id=other, device_id_type=MESH)
    own_p.wait()
    for copy in own_d:
        copy.wait()
    pl.semaphore_wait(barrier, len(partners))

    def remote(src, dst, send, recv, device):
        return pltpu.make_async_remote_copy(
            src_ref=src, dst_ref=dst, send_sem=send, recv_sem=recv, device_id=device, device_id_type=MESH
        )

    delta = lax.rem(r // 4 + NZ - z, NZ)
    delta_across = lax.rem(delta + 4, NZ)

    def is_in(values, where):
        hit = jnp.int32(0)
        for v in values:
            hit = hit + jnp.where(where == v, 1, 0)
        return hit

    AWAY = ((4, 5, 6, 7), (3, 4, 5, 6), (2, 3, 4, 5), (1, 2, 3, 4))
    HELPER = (down, down2, up2, up)
    HELP = (HELP1, HELP2, HELP2, HELP1)
    TURN = (7, 6, -1, -1)

    def moves(role, part, where):
        away = is_in(AWAY[role], where)
        turn = is_in((TURN[role],), where)
        turned = turn if part == 0 else 1 - turn
        return away * turned, away * (1 - turned)

    def help_copy(role, part, staged):
        src = stage.at[role, part] if staged else pown.at[part, freq(role)]
        n = 1 if staged else 0
        group = HELP[role]
        return remote(
            src, pall.at[group, part, r], help_send.at[n, role, part], help_recv.at[group, part], HELPER[role]
        )

    def stage_copy(role, part):
        return remote(
            pown.at[part, freq(role)], stage.at[role, part], stage_send.at[role, part], stage_recv.at[role, part], across
        )

    def own_copy(role):
        if role == 0:
            mine, dy = is_in((0, 1, 2, 3), delta), 0
        elif role == 3:
            mine, dy = is_in((0, 5, 6, 7), delta), is_in((0,), delta) * 2
        elif role == 1:
            mine, dy = is_in((7, 0, 1, 2), delta), 0
        else:
            mine = is_in((6, 7, 0, 1), delta)
            dy = is_in((7,), delta) * 3 + is_in((0,), delta) * 2 + is_in((1,), delta)
        group = OWN03 if role in (0, 3) else OWN12
        target = rec_of(x, lax.rem(y + dy, 4), c)
        src, dst = pown.at[:, freq(role)], pall.at[group, :, target]
        stays = mine * jnp.where(dy == 0, 1, 0)
        leaves = mine * jnp.where(dy == 0, 0, 1)

        def local():
            return pltpu.make_async_copy(src, dst, own_recv.at[group])

        def away():
            return remote(src, dst, own_send.at[role], own_recv.at[group], (z, target))

        return stays, leaves, local, away

    def when(condition, action):
        @pl.when(condition == 1)
        def _():
            action()

    def place_direct():
        for role in (3, 0, 2, 1):
            for part in (0, 1):
                when(moves(role, part, delta)[1], lambda: help_copy(role, part, False).start())

    def place_across():
        for role in (3, 0, 2, 1):
            for part in (1, 0):
                when(moves(role, part, delta)[0], lambda: stage_copy(role, part).start())

    def place_own(roles):
        for role in roles:
            stays, leaves, local, away = own_copy(role)
            when(stays, lambda: local().start())
            when(leaves, lambda: away().start())

    def place_staged():
        for role in (3, 0, 2, 1):
            for part in (1, 0):

                def pass_on():
                    stage_copy(role, part).wait_recv()
                    help_copy(role, part, True).start()

                when(moves(role, part, delta_across)[0], pass_on)

    def place_sent():
        for role in range(4):
            for part in (0, 1):
                when(moves(role, part, delta)[1], lambda: help_copy(role, part, False).wait_send())
                when(moves(role, part, delta)[0], lambda: stage_copy(role, part).wait_send())
                when(moves(role, part, delta_across)[0], lambda: help_copy(role, part, True).wait_send())
            leaves, away = own_copy(role)[1], own_copy(role)[3]
            when(leaves, lambda: away().wait_send())

    seen = []

    def piece_wait(group, part):
        if group in (HELP1, HELP2):
            ref = pall.at[group, part, r]
            remote(ref, ref, help_send.at[0, 0, part], help_recv.at[group, part], sibling).wait_recv()
        elif group not in seen:
            seen.append(group)
            ref = pall.at[group, :, r]
            pltpu.make_async_copy(ref, ref, own_recv.at[group]).wait()

    def d_copy(role, pos, part, upwards):
        f = freq(role)
        src = dall.at[f, pos, part]
        way = 0 if upwards else 1
        return remote(src, dall.at[f, pos, part], d_send.at[way], d_recv.at[f, pos, part], up if upwards else down)

    def d_wait(role, pos):
        f = freq(role)
        for part in (0, 1):
            ref = dall.at[f, pos, part]
            remote(ref, ref, d_send.at[0], d_recv.at[f, pos, part], up).wait_recv()

    def d_forward(role, pos, upwards):
        d_wait(role, pos)
        for part in (0, 1):
            d_copy(role, pos, part, upwards).start()

    def d_own(i):
        for part in (0, 1):
            d_copy(i, i, part, True).start()
            d_copy(3 - i, 3 - i, part, False).start()

    def slot(part, a, b):
        return rec(a, b) if part == 0 else rec(b, a)

    def p_copy(group, part, a, b, index, device, half=None):
        ref = pall.at[group, part, slot(part, a, b)]
        if half is not None:
            ref = ref.at[pl.ds(half * 128, 128)]
        return remote(ref, ref, p_send.at[group, part], p_recv.at[group, part, index], device)

    def share(group, part, a, b):
        ref = pall.at[group, part, slot(part, a, b)]
        remote(ref, ref, sib_send.at[group], sib_recv.at[group], sibling).start()

    def first(part):
        return sides[part]

    def second(part):
        return sides[1 - part]

    LINE = (0, -1, 1, 2)

    def stage1(group, parts=(0, 1)):
        for part in parts:
            piece_wait(group, part)
            for way in (0, 1):
                p_copy(group, part, 0, 0, way, first(part)[way]).start()
            for way in (0, 1):
                p_copy(group, part, 0, 0, 4 + way, second(part)[way]).start()
            share(group, part, 0, 0)

    def stage2(group, parts=(0, 1)):
        for way in (0, 1):
            a = LINE[1 + way]
            for part in parts:
                p_copy(group, part, a, 0, way, sibling).wait_recv()
                p_copy(group, part, a, 0, 2 + way, first(part)[way], half=way).start()
                for turn in (0, 1):
                    p_copy(group, part, a, 0, 4 + 4 * (1 + way) + turn, second(part)[turn]).start()
                share(group, part, a, 0)

    def stage2b(group, parts=(0, 1)):
        for part in parts:
            for way in (0, 1):
                p_copy(group, part, 2, 0, 2 + way, sibling, half=way).wait_recv()
            for turn in (0, 1):
                p_copy(group, part, 2, 0, 16 + turn, second(part)[turn]).start()
            share(group, part, 2, 0)

    def stage3(group, parts=(0, 1)):
        for i in range(4):
            for way in (0, 1):
                b = LINE[1 + way]
                for part in parts:
                    p_copy(group, part, LINE[i], b, 4 + 4 * i + way, sibling).wait_recv()
                    p_copy(group, part, LINE[i], b, 6 + 4 * i + way, second(part)[way], half=way).start()
                    share(group, part, LINE[i], b)

    def stage4(group, parts=(0, 1)):
        for i in range(4):
            for part in parts:
                for way in (0, 1):
                    p_copy(group, part, LINE[i], 2, 6 + 4 * i + way, sibling, half=way).wait_recv()
                share(group, part, LINE[i], 2)

    def shared(group):
        ref = pall.at[group, :, pl.ds(0, NQ)]
        return remote(ref, ref, sib_send.at[group], sib_recv.at[group], sibling)

    def home(group, part, role, pos):
        if group in (OWN12, OWN03):
            return plane(((0, 1, 2, 3), (-1, 0, 1, 2), (-2, -3, 4, 3), (-3, -2, -1, 4))[role][pos])
        if role == 0:
            return plane(pos if part == 0 else pos + 4)
        return plane((-3, -2, -1, 4)[pos] if part == 0 else (1, 2, 3, 0)[pos])

    def product(group, role, pos):
        f = freq(role)
        left = []
        for part in (0, 1):
            base = home(group, part, role, pos) * 4
            left.append(jnp.concatenate([pall[group, part, base + i] for i in range(4)], axis=1))
        re, im = dall[f, pos, 0], dall[f, pos, 1]
        u = jnp.dot(left[0], jnp.concatenate([re, im], axis=1), preferred_element_type=jnp.float32)
        v = jnp.dot(left[1], jnp.concatenate([im, re], axis=1), preferred_element_type=jnp.float32)
        return u[:, :128] - v[:, :128], u[:, 128:] + v[:, 128:]

    def help_step(group, role, n):
        index = (0 if role == 0 else 1) + (0 if group == HELP1 else 2)
        for part, value in enumerate(product(group, role, n if role == 0 else 3 - n)):
            if n == 0:
                cpart[index, part] = value
            else:
                cpart[index, part] += value

    waited = []

    def d_once(role, pos):
        if (role, pos) not in waited:
            waited.append((role, pos))
            d_wait(role, pos)

    def help_first(group, n):
        if n == 0:
            shared(group).wait_recv()
        for role in (0, 3):
            if n > 0:
                d_once(role, n if role == 0 else 3 - n)
            help_step(group, role, n)

    def help_last(group):
        for role in (0, 3):
            d_once(role, 3 - role)
            help_step(group, role, 3)
            index = (0 if role == 0 else 1) + (0 if group == HELP1 else 2)
            f = freq(role)
            near, far = (down, down2) if role == 0 else (up, up2)
            for part in (0, 1):
                remote(
                    cpart.at[index, part], other_ref.at[part, f], c_send.at[index], c_recv.at[f, part],
                    near if group == HELP1 else far,
                ).start()

    def out_copy(role):
        f = freq(role)
        return pltpu.make_async_copy(total.at[:, f], own_ref.at[:, f], local_sem.at[role])

    def own_block(group):
        shared(group).wait_recv()
        for role in (0, 3) if group == OWN03 else (1, 2):
            f = freq(role)
            for pos in range(4):
                for part, value in enumerate(product(group, role, pos)):
                    if pos == 0:
                        total[part, f] = value
                    else:
                        total[part, f] += value
            out_copy(role).start()

    place_across()
    place_direct()
    place_own((0, 3))
    place_own((1, 2))
    d_own(0)
    stage1(OWN03, (1,))
    stage1(HELP1, (0,))
    place_staged()
    stage1(OWN03, (0,))
    stage1(OWN12, (1,))
    stage1(HELP2, (0,))
    d_own(1)
    d_own(2)
    d_forward(1, 0, True)
    d_forward(2, 3, False)
    stage1(HELP1, (1,))
    stage1(HELP2, (1,))
    stage2(HELP2, (0,))
    stage2(HELP1, (1,))
    stage2(HELP2, (1,))
    stage2b(HELP2, (0,))
    stage2(HELP1, (0,))
    stage2b(HELP2, (1,))
    d_forward(2, 1, True)
    d_forward(1, 2, False)
    stage2b(HELP1, (1,))
    stage3(HELP2, (0,))
    stage2b(HELP1, (0,))
    stage3(HELP2, (1,))
    stage3(HELP1, (1,))
    stage3(HELP1, (0,))
    d_forward(2, 0, True)
    d_forward(1, 3, False)
    stage2(OWN03, (0,))
    stage2(OWN03, (1,))
    stage4(HELP2, (0,))
    stage4(HELP2, (1,))
    stage4(HELP1, (1,))
    stage4(HELP1, (0,))
    stage2b(OWN03, (0,))
    stage1(OWN12, (0,))
    help_first(HELP2, 0)
    help_first(HELP2, 1)
    stage2(OWN12, (1,))
    help_first(HELP2, 2)
    stage3(OWN03, (0,))
    stage2b(OWN03, (1,))
    stage2(OWN12, (0,))
    help_last(HELP2)
    stage2b(OWN12, (1,))
    help_first(HELP1, 0)
    help_first(HELP1, 1)
    help_first(HELP1, 2)
    stage3(OWN03, (1,))
    help_last(HELP1)
    stage2b(OWN12, (0,))
    stage3(OWN12, (1,))
    stage3(OWN12, (0,))
    stage4(OWN03, (1,))
    stage4(OWN03, (0,))
    stage4(OWN12, (1,))
    stage4(OWN12, (0,))
    own_block(OWN03)
    own_block(OWN12)
    for group in range(4):
        shared(group).wait_send()
        for part in (0, 1):
            ref = pall.at[group, part, pl.ds(0, NQ - 1)]
            remote(ref, ref, p_send.at[group, part], p_recv.at[group, part, 0], sibling).wait_send()
    for way in (0, 1):
        ref = dall.at[pl.ds(0, 3), pl.ds(0, 2)]
        remote(ref, ref, d_send.at[way], d_recv.at[0, 0, 0], up).wait_send()
    place_sent()

    for role in (0, 3, 1, 2):
        f = freq(role)
        out_copy(role).wait()
        for part in (0, 1):
            ref = other_ref.at[part, f]
            remote(ref, ref, c_send.at[0], c_recv.at[f, part], up).wait_recv()
    for index in range(4):
        remote(cpart.at[index], cpart.at[index], c_send.at[index], c_recv.at[0, 0], up).wait_send()


def shards(primaries, recorded):
    own, other = pl.pallas_call(
        kernel,
        out_shape=(jax.ShapeDtypeStruct((2, F, 256, 128), jnp.float32),) * 2,
        in_specs=[pl.BlockSpec(memory_space=pl.ANY)] * 2,
        out_specs=(pl.BlockSpec(memory_space=pl.ANY),) * 2,
        scratch_shapes=[
            pltpu.VMEM((2, F, 256, 128), jnp.bfloat16),
            pltpu.VMEM((4, 2, 2 * NQ, 256, 128), jnp.bfloat16),
            pltpu.VMEM((F, 4, 2, 512, 128), jnp.bfloat16),
            pltpu.VMEM((4, 2, 256, 128), jnp.float32),
            pltpu.VMEM((2, F, 256, 128), jnp.float32),
            pltpu.VMEM((4, 2, 256, 128), jnp.bfloat16),
            pltpu.SemaphoreType.DMA((2, 4, 2)),
            pltpu.SemaphoreType.DMA((4, 2)),
            pltpu.SemaphoreType.DMA((4, 2)),
            pltpu.SemaphoreType.DMA((4, 2)),
            pltpu.SemaphoreType.DMA((4,)),
            pltpu.SemaphoreType.DMA((4,)),
            pltpu.SemaphoreType.DMA((4, 2)),
            pltpu.SemaphoreType.DMA((4, 2, 20)),
            pltpu.SemaphoreType.DMA((4,)),
            pltpu.SemaphoreType.DMA((4,)),
            pltpu.SemaphoreType.DMA((2,)),
            pltpu.SemaphoreType.DMA((F, 4, 2)),
            pltpu.SemaphoreType.DMA((4,)),
            pltpu.SemaphoreType.DMA((F, 2)),
            pltpu.SemaphoreType.DMA((5,)),
        ],
        compiler_params=pltpu.CompilerParams(
            collective_id=0, has_side_effects=True, vmem_limit_bytes=56 * 1024 * 1024
        ),
        cost_estimate=pl.CostEstimate(flops=4294967296, bytes_accessed=3 << 20, transcendentals=0),
    )(primaries, recorded)
    return own + other


def solution(mesh):
    placed = (P(None, None, "shot", "rec"), P(None, None, "shot", "rec"))
    return jax.shard_map(
        shards, mesh=mesh, in_specs=placed, out_specs=P(None, None, "shot", "rec"), check_vma=False
    )
```
